32 devices in a mesh: groups: 2 (over y), ep: 4 (over z), tp: 4 (over x, core).
Axes of the slice: x: 2, y: 2, z: 4, core: 2. Of those that a mesh axis runs over, the one named last changes fastest.
Arguments:
- tokens: bfloat16 [2, 512, 4096], P(None, ('groups', 'ep')), parts along dimension 1, may hold values from -6 to 6
- expert_ids: int32 [2, 512, 2], P(None, ('groups', 'ep')), parts along dimension 1, may hold values from 0 to 1, all different within a row
- gate_weights: float32 [2, 512, 2], P(None, ('groups', 'ep')), parts along dimension 1, may hold values from 0.05 to 1
- replica_pick: int32 [2, 512, 2], P(None, ('groups', 'ep')), parts along dimension 1, may hold values from 0 to 3
- placement: int32 [2, 4], replicated, may hold values from 0 to 1, as said below
- slot_limit: int32 [4], replicated, may hold values from 20 to 40, as said below
- expert_weights: bfloat16 [4, 3, 1536, 4096], P('ep', None, 'tp'), as said below
Outputs:
- layer_out: bfloat16 [2, 512, 4096], P(None, ('groups', 'ep'), 'tp'), parts along dimension 1
The draws below stay inside these ranges and needn't reach their ends.
There are 2 independent parts, one for each index of `groups`. The reference program is written for one: setup_inputs(seed, part) draws one part's arguments, and reference() takes and returns one part's arrays. A program takes and returns all parts, laid end to end along the dimension named above; an argument that names none is the same for every part. Nothing has to cross between parts.
Inputs may be any that keep to these rules, and one draw needn't show every extreme that they name: `expert_ids`: each row names 2 different experts, and every expert is named somewhere. `placement`: row 0 is the old and row 1 the new slot-to-expert table. In each table every expert is held by one or more slots, and exactly 2 slots hold another expert in row 1 than in row 0. `slot_limit`: some slot has capacity exactly 40. `expert_weights`: slots that hold the same expert in the old table hold equal weights.
All inputs are finite; a program needn't handle non-finite values.
Results may differ from the reference program's by a relative error of at most 0.015.
Values may be sent and summed in bfloat16 or wider, within the bound.
No kernel may reach another device: no remote copies, remote signals or barrier semaphores. Data moves between devices by JAX's collectives and lax.ppermute only.
A program may use at most 128 MiB of HBM per device.

```python
import math
import jax
import jax.numpy as jnp
from jax import lax

D = 4096
FF = 1536
TOK_DEV = 64
SLOTS = 4
REDUND = 2
EXPERTS = 2
TOP = 2
CAP = 40
TOKENS = 256
N_EP = 4
N_TP = 4


def tables(table_key):
    key_first, key_second, key_third = jax.random.split(table_key, 3)
    base_slot = jax.random.randint(key_first, (), 0, SLOTS).astype(jnp.int32)
    expert_order = jax.random.permutation(key_second, EXPERTS).astype(jnp.int32)
    position = jnp.arange(EXPERTS, dtype=jnp.int32)
    primary_slots = ((base_slot + REDUND + position) % SLOTS).astype(jnp.int32)
    old_table = jnp.zeros((SLOTS,), jnp.int32).at[primary_slots].set(expert_order)
    far_position = SLOTS // 2 + 1 - REDUND
    near_position = EXPERTS - 1
    if far_position == near_position:
        free_count = EXPERTS - 1
    else:
        free_count = EXPERTS - 2
    free_draw = jax.random.randint(key_third, (REDUND,), 0, free_count).astype(jnp.int32)
    free_position = jnp.where(free_draw >= far_position, free_draw + 1, free_draw).astype(jnp.int32)
    old_extra = expert_order[free_position]
    source_position = jnp.full((REDUND,), near_position, jnp.int32).at[1].set(far_position)
    new_extra = expert_order[source_position]
    target_slots = ((base_slot + jnp.arange(REDUND, dtype=jnp.int32)) % SLOTS).astype(jnp.int32)
    new_table = old_table.at[target_slots].set(new_extra)
    old_table = old_table.at[target_slots].set(old_extra)
    return (old_table, new_table)


def draw_placement(key, part):
    old_table, new_table = tables(jax.random.fold_in(key, 11))
    return jnp.stack([old_table, new_table]).astype(jnp.int32)


def draw_expert_weights(key, part):
    old_table, new_table = tables(jax.random.fold_in(key, 11))
    normal_draw = jax.random.normal(jax.random.fold_in(key, 12), (EXPERTS, 3, FF, D), jnp.float32)
    scales = jnp.array([D ** (-0.5), D ** (-0.5), FF ** (-0.5)], jnp.float32)
    scaled = normal_draw * scales[None, :, None, None]
    return scaled[old_table].astype(jnp.bfloat16)


def draw_slot_limit(key, part):
    inner_key = jax.random.fold_in(key, 13)
    limits = jax.random.randint(inner_key, (SLOTS,), CAP // 2, CAP + 1)
    filled = jax.random.randint(jax.random.fold_in(inner_key, 1), (), 0, SLOTS)
    return jnp.where(jnp.arange(SLOTS) == filled, CAP, limits).astype(jnp.int32)


def plant(entries, own_key, smallest, largest):
    longest = entries.shape.index(max(entries.shape))
    spots = []
    for shift in (0, 1):
        where = [jax.random.randint(jax.random.fold_in(own_key, axis), (), 0, length) for axis, length in enumerate(entries.shape)]
        where[longest] = (where[longest] + shift) % entries.shape[longest]
        spots.append(tuple(where))
    return entries.at[spots[0]].set(smallest).at[spots[1]].set(largest)


def level_of(key, dims, shards, smallest, largest):
    loudness = 1.0
    for axis_at, shards_of in shards:
        steps = jax.random.uniform(jax.random.fold_in(jax.random.fold_in(key, 6), axis_at), (shards_of,), jnp.float32, smallest / len(shards), largest / len(shards))
        loudness = loudness * jnp.repeat(jnp.exp(steps), dims[axis_at] // shards_of).reshape((-1,) + (1,) * (len(dims) - 1 - axis_at))
    return loudness


def choose_distinct(stream_key, rows, number_of, top, lift):
    sequence = jax.random.permutation(jax.random.fold_in(stream_key, 1), number_of)
    boost = sequence
    for power in range(3):
        boost = boost * boost // number_of
    boost = boost * lift // number_of
    tickets = jax.random.randint(jax.random.fold_in(stream_key, 2), (rows, number_of), 0, 4096) + boost
    fixed_rows = jax.random.permutation(jax.random.fold_in(stream_key, 3), rows)[jnp.arange(number_of) % rows]
    tickets = jnp.where(jnp.arange(rows)[:, None] == fixed_rows[None, :], 1 << 14, tickets)
    merit = tickets * number_of + jnp.arange(number_of)
    return lax.top_k(merit.astype(jnp.int32), top)[1].astype(jnp.int32)


def centred(rng, extent, scale, reach, cuts=(), kind=jnp.bfloat16):
    gain = level_of(rng, extent, cuts, -0.22, 0.18) if cuts else 1.0
    values = jax.random.normal(rng, extent, jnp.float32) * scale * gain
    return jnp.minimum(jnp.maximum(values, -reach), reach).astype(kind)


def setup_inputs(seed: int = 0, part: int = 0) -> dict:
    keys = jax.random.split(jax.random.key(seed), 8)
    part_splits = jax.random.split(jax.random.fold_in(keys[7], part), 8)
    tokens = centred(part_splits[0], (2, TOKENS, D), 1.0, 6.0, ((1, 4),))
    expert_ids = choose_distinct(part_splits[1], 2 * TOKENS, EXPERTS, TOP, 12000).reshape((2, TOKENS, TOP))
    gate_weights = jnp.clip(jnp.exp(math.log(1.0) - 2.9957323 * jax.random.uniform(part_splits[2], (2, TOKENS, TOP), jnp.float32) ** level_of(part_splits[2], (2, TOKENS, TOP), ((1, 4),), -0.2, 0.2)), 0.05, 1.0)
    replica_pick = plant(jax.random.randint(part_splits[3], (2, TOKENS, TOP), 0, 4), jax.random.fold_in(part_splits[3], 1), 0, 3).astype(jnp.int32)
    placement = draw_placement(jax.random.fold_in(keys[7], 71), part)
    slot_limit = draw_slot_limit(jax.random.fold_in(keys[7], 71), part)
    expert_weights = draw_expert_weights(jax.random.fold_in(keys[7], 71), part)
    return dict(tokens=tokens, expert_ids=expert_ids, gate_weights=gate_weights, replica_pick=replica_pick, placement=placement, slot_limit=slot_limit, expert_weights=expert_weights)


def slot_choice(slot_table, chosen_ids, pick_values, slot_count):
    slot_range = jnp.arange(slot_count, dtype=jnp.int32)
    holders = (slot_table[None, None, :] == chosen_ids[:, :, None]).astype(jnp.int32)
    holder_count = jnp.sum(holders, axis=2)
    earlier = jnp.cumsum(holders, axis=2) - holders
    wanted = pick_values % holder_count
    matched = holders * (earlier == wanted[:, :, None]).astype(jnp.int32)
    return jnp.sum(matched * slot_range[None, None, :], axis=2)


def placements(slot_table, limits, chosen_ids, pick_values, block_rows, capacity):
    slot_count = slot_table.shape[0]
    chosen = slot_choice(slot_table, chosen_ids, pick_values, slot_count)
    row_count, top_count = chosen.shape
    blocked = chosen.reshape(row_count // block_rows, block_rows * top_count)
    onehot = (blocked[:, :, None] == jnp.arange(slot_count, dtype=jnp.int32)[None, None, :]).astype(jnp.int32)
    ranked = jnp.sum(onehot * (jnp.cumsum(onehot, axis=1) - onehot), axis=2)
    allowed = jnp.sum(onehot * limits[None, None, :], axis=2)
    located = jnp.where(ranked < allowed, blocked * capacity + ranked, slot_count * capacity)
    return located.reshape(row_count, top_count)


def expert_apply(inputs, weights):
    gate_proj = jnp.dot(inputs, weights[0].T, preferred_element_type=jnp.float32)
    upward = jnp.dot(inputs, weights[1].T, preferred_element_type=jnp.float32)
    hidden = (jax.nn.silu(gate_proj) * upward).astype(jnp.bfloat16)
    group_size = hidden.shape[1] // N_TP
    summed = jnp.zeros((inputs.shape[0], inputs.shape[1]), jnp.float32)
    for member in range(N_TP):
        lower = member * group_size
        partial_out = jnp.dot(hidden[:, lower:lower + group_size], weights[2, lower:lower + group_size],
                              preferred_element_type=jnp.float32).astype(jnp.bfloat16)
        partial_out = lax.optimization_barrier(partial_out)
        summed = summed + partial_out.astype(jnp.float32)
    return summed.astype(jnp.bfloat16)


def run_span(span_rows, chosen_ids, weight_values, pick_values, slot_table, limits, weights):
    located = placements(slot_table, limits, chosen_ids, pick_values, TOK_DEV, CAP)
    token_index = jnp.arange(TOKENS, dtype=jnp.int32)
    source_block = token_index // TOK_DEV
    kept_mask = located < SLOTS * CAP
    slot_index = located // CAP
    rank_index = located % CAP
    buffer_index = jnp.where(kept_mask, slot_index * (N_EP * CAP) + source_block[:, None] * CAP + rank_index,
                             SLOTS * N_EP * CAP).astype(jnp.int32)
    token_source = jnp.full((SLOTS * N_EP * CAP + 1,), TOKENS, jnp.int32)
    spread = jnp.broadcast_to(token_index[:, None], buffer_index.shape).reshape(-1)
    token_source = token_source.at[buffer_index.reshape(-1)].set(spread)[:-1]
    padded_rows = jnp.concatenate([span_rows, jnp.zeros((1, D), jnp.bfloat16)])
    buffers = padded_rows[token_source].reshape(SLOTS, N_EP * CAP, D)
    outputs = lax.map(lambda operands: expert_apply(operands[0], operands[1]), (buffers, weights))
    flat_out = jnp.concatenate([outputs.reshape(SLOTS * N_EP * CAP, D), jnp.zeros((1, D), jnp.bfloat16)])
    combined = jnp.zeros((TOKENS, D), jnp.float32)
    for member in range(TOP):
        combined = combined + weight_values[:, member, None] * flat_out[buffer_index[:, member]].astype(jnp.float32)
    return combined.astype(jnp.bfloat16)


def reference(tokens, expert_ids, gate_weights, replica_pick, placement, slot_limit, expert_weights):
    first_out = run_span(tokens[0], expert_ids[0], gate_weights[0], replica_pick[0], placement[0],
                          slot_limit, expert_weights)
    slot_range = jnp.arange(SLOTS, dtype=jnp.int32)
    matches = placement[0][None, :] == placement[1][:, None]
    sources = jnp.min(jnp.where(matches, slot_range[None, :], SLOTS), axis=1).astype(jnp.int32)
    relocated = expert_weights[sources]
    second_out = run_span(tokens[1], expert_ids[1], gate_weights[1], replica_pick[1], placement[1],
                           slot_limit, relocated)
    return jnp.stack([first_out, second_out])
```

```python
import functools

import jax
import jax.numpy as jnp
from jax import lax
from jax.experimental import pallas as pl
from jax.experimental.pallas import tpu as pltpu
from jax.sharding import PartitionSpec as P

VMEM_LIMIT = 32 * 1024 * 1024
CONTRACT_LAST = (((1,), (1,)), ((), ()))


def routes(placement, limits, chosen_ids, pick_values, gates):
    spans, rows, top = chosen_ids.shape
    slots = placement.shape[1]
    slot_range = jnp.arange(slots, dtype=jnp.int32)
    same = placement[:, :, None] == placement[:, None, :]
    before = slot_range[None, :] < slot_range[:, None]
    turn = jnp.sum((same & before).astype(jnp.int32), axis=2)
    flat_ids = chosen_ids.reshape(spans, rows * top)
    holders = flat_ids[:, :, None] == placement[:, None, :]
    count = jnp.sum(holders.astype(jnp.int32), axis=2)
    wanted = pick_values.reshape(spans, rows * top) % count
    onehot = holders & (turn[:, None, :] == wanted[:, :, None])
    slot = jnp.sum(jnp.where(onehot, slot_range, 0), axis=2)
    limit = jnp.sum(jnp.where(onehot, limits, 0), axis=2)
    order = jnp.arange(rows * top, dtype=jnp.int32)
    ahead = (slot[:, :, None] == slot[:, None, :]) & (order[None, :] < order[:, None])
    rank = jnp.sum(ahead.astype(jnp.int32), axis=2)
    kept = rank < limit
    shape = (spans, rows, top)
    return (
        slot.reshape(shape),
        rank.reshape(shape),
        jnp.where(kept.reshape(shape), gates, 0.0),
        kept.reshape(shape),
    )


def in_vmem(count):
    return [pl.BlockSpec(memory_space=pltpu.VMEM)] * count


def with_core(count):
    return [pl.BlockSpec(memory_space=pltpu.SMEM)] + in_vmem(count)


def params():
    return pltpu.CompilerParams(vmem_limit_bytes=VMEM_LIMIT)


def cost(rows, width, units):
    return pl.CostEstimate(
        flops=2 * rows * width * units, bytes_accessed=2 * rows * width, transcendentals=0
    )


def in_hbm():
    return pl.BlockSpec(memory_space=pltpu.HBM)


def take_kernel(span, core_ref, from_ref, out_ref, sems):
    chips = core_ref.shape[0]
    part = out_ref.shape[1] // chips
    copies = []
    for chip in range(chips):
        at = pl.multiple_of((2 * chip + core_ref[chip]) * part, part)
        to = out_ref.at[:, chip * part : (chip + 1) * part]
        copies.append(pltpu.make_async_copy(from_ref.at[span, :, pl.ds(at, part)], to, sems.at[chip]))
        copies[-1].start()
    for copy in copies:
        copy.wait()


def take(core, tokens, span):
    chips = core.shape[0]
    rows, width = tokens.shape[1:]
    return pl.pallas_call(
        functools.partial(take_kernel, span),
        out_shape=jax.ShapeDtypeStruct((rows, width // 2), jnp.bfloat16),
        in_specs=[pl.BlockSpec(memory_space=pltpu.SMEM), in_hbm()],
        out_specs=in_vmem(1)[0],
        scratch_shapes=[pltpu.SemaphoreType.DMA((chips,))],
        compiler_params=params(),
        cost_estimate=cost(rows, width, 1),
    )(core, tokens)


def pack_kernel(core_ref, choose_ref, rows_ref, own_ref, *out_refs):
    chips = core_ref.shape[0]
    count = own_ref.shape[0]
    part = own_ref.shape[1] // (2 * chips)
    first = core_ref[0] == 0
    choose = choose_ref[...]
    for chip in range(chips):
        of = 2 * chip * part
        low = jnp.dot(
            choose, rows_ref[:, of : of + part], preferred_element_type=jnp.float32
        )
        high = jnp.dot(
            choose, rows_ref[:, of + part : of + 2 * part], preferred_element_type=jnp.float32
        )
        own_ref[:, of : of + part] = low[:count].astype(jnp.bfloat16)
        own_ref[:, of + part : of + 2 * part] = high[:count].astype(jnp.bfloat16)
        sent = jnp.where(first, low, high)
        for index, out_ref in enumerate(out_refs):
            at = (index + 1) * count
            out_ref[:, chip * part : (chip + 1) * part] = sent[at : at + count].astype(jnp.bfloat16)


def pack(core, choose, rows, slots):
    count = choose.shape[0] // slots
    width = rows.shape[1]
    outs = [jax.ShapeDtypeStruct((count, width), jnp.bfloat16)]
    outs += [jax.ShapeDtypeStruct((count, width // 2), jnp.bfloat16)] * (slots - 1)
    own, *others = pl.pallas_call(
        pack_kernel,
        out_shape=outs,
        in_specs=with_core(2),
        out_specs=in_vmem(slots),
        compiler_params=params(),
        cost_estimate=cost(choose.shape[0], choose.shape[1], width),
    )(core, choose, rows)
    return own, others


def load_kernel(columns_ref, from_ref, up_ref, down_ref, sent_ref, sems):
    parts = up_ref.shape[0]
    chips = down_ref.shape[0]
    part = up_ref.shape[3]
    copies = []
    for chip in range(chips):
        for side, to_ref in enumerate((sent_ref, down_ref)):
            at = pl.multiple_of(columns_ref[2 * side, chip] * part, part)
            copies.append(
                pltpu.make_async_copy(
                    from_ref.at[0, 2, :, pl.ds(at, part)], to_ref.at[chip], sems.at[2 * chip + side]
                )
            )
    for index in range(parts):
        copies.append(
            pltpu.make_async_copy(
                from_ref.at[0, 0:2, :, index * part : (index + 1) * part],
                up_ref.at[index],
                sems.at[parts + index],
            )
        )
    for copy in copies:
        copy.start()
    for copy in copies:
        copy.wait()


def load(columns, weights):
    chips = columns.shape[1]
    units, width = weights.shape[2:]
    part = width // (2 * chips)
    return pl.pallas_call(
        load_kernel,
        out_shape=[
            pltpu.VMEM((2 * chips, 2, units, part), jnp.bfloat16),
            pltpu.VMEM((chips, units, part), jnp.bfloat16),
            jax.ShapeDtypeStruct((chips, units, part), jnp.bfloat16),
        ],
        in_specs=[pl.BlockSpec(memory_space=pltpu.SMEM), in_hbm()],
        out_specs=in_vmem(3),
        scratch_shapes=[pltpu.SemaphoreType.DMA((4 * chips,))],
        compiler_params=params(),
        cost_estimate=cost(3 * units, width, 1),
    )(columns, weights)


def up_kernel(core_ref, own_ref, *refs):
    *piece_refs, weight_ref, hidden_ref, rows_ref = refs
    chips = core_ref.shape[0]
    count = len(piece_refs) // 2
    part = own_ref.shape[1] // (2 * chips)
    first = core_ref[0] == 0
    gate = upward = 0.0
    for index in range(2 * chips):
        chip, core = index // 2, index % 2
        column = slice(index * part, (index + 1) * part)
        of = slice(chip * part, (chip + 1) * part)
        values = [own_ref[:, column]]
        for piece in range(count):
            own, other = piece_refs[piece][:, of], piece_refs[count + piece][:, of]
            values.append(
                jnp.where(first, own, other) if core == 0 else jnp.where(first, other, own)
            )
        if all(value.shape[0] % 16 == 0 for value in values):
            at = 0
            for value in values:
                rows_ref[at : at + value.shape[0]] = value
                at += value.shape[0]
        else:
            joined = jnp.concatenate([value.astype(jnp.float32) for value in values])
            rows_ref[...] = joined.astype(jnp.bfloat16)
        rows = rows_ref[...]
        gate += lax.dot_general(
            rows, weight_ref[index, 0], CONTRACT_LAST, preferred_element_type=jnp.float32
        )
        upward += lax.dot_general(
            rows, weight_ref[index, 1], CONTRACT_LAST, preferred_element_type=jnp.float32
        )
    hidden_ref[...] = (gate / (1.0 + jnp.exp(-gate)) * upward).astype(jnp.bfloat16)


def up(core, own, own_pieces, other_pieces, weights):
    total, width = own.shape[0] + sum(piece.shape[0] for piece in own_pieces), own.shape[1]
    units, part = weights.shape[2:]
    return pl.pallas_call(
        up_kernel,
        out_shape=jax.ShapeDtypeStruct((total, units), jnp.bfloat16),
        in_specs=with_core(2 * len(own_pieces) + 2),
        out_specs=in_vmem(1)[0],
        scratch_shapes=[pltpu.VMEM((total, part), jnp.bfloat16)],
        compiler_params=params(),
        cost_estimate=cost(total, width, 2 * units),
    )(core, own, *own_pieces, *other_pieces, weights)


def down_kernel(columns_ref, hidden_ref, other_hidden_ref, weight_ref, other_ref, *out_refs):
    hidden, other_hidden = hidden_ref[...], other_hidden_ref[...]
    for shift, out_ref in enumerate(out_refs):
        total = jnp.dot(hidden, weight_ref[shift], preferred_element_type=jnp.float32)
        total += jnp.dot(
            other_hidden, other_ref[columns_ref[1, shift]], preferred_element_type=jnp.float32
        )
        out_ref[...] = total.astype(jnp.bfloat16)


def down(columns, hidden, other_hidden, weights, other_weights):
    chips, units, part = other_weights.shape
    rows = hidden.shape[0]
    return pl.pallas_call(
        down_kernel,
        out_shape=[jax.ShapeDtypeStruct((rows, part), jnp.bfloat16)] * chips,
        in_specs=with_core(4),
        out_specs=in_vmem(chips),
        compiler_params=params(),
        cost_estimate=cost(rows, 2 * units, chips * part),
    )(columns, hidden, other_hidden, weights, other_weights)


def unpack_kernel(weight_ref, *refs):
    *piece_refs, out_ref = refs
    rows = jnp.concatenate([ref[...].astype(jnp.float32) for ref in piece_refs])
    rows = rows.astype(jnp.bfloat16)
    weight = weight_ref[...]
    high = weight.astype(jnp.bfloat16)
    low = (weight - high.astype(jnp.float32)).astype(jnp.bfloat16)
    total = jnp.dot(high, rows, preferred_element_type=jnp.float32)
    total += jnp.dot(low, rows, preferred_element_type=jnp.float32)
    out_ref[...] = total.astype(jnp.bfloat16)


def unpack(weight, pieces):
    rows, part = weight.shape[0], pieces[0].shape[1]
    return pl.pallas_call(
        unpack_kernel,
        out_shape=jax.ShapeDtypeStruct((rows, part), jnp.bfloat16),
        in_specs=in_vmem(1 + len(pieces)),
        out_specs=in_vmem(1)[0],
        compiler_params=params(),
        cost_estimate=cost(rows, weight.shape[1], part),
    )(weight, *pieces)


def per_device(
    tokens, expert_ids, gate_weights, replica_pick, placement, slot_limit, expert_weights
):
    spans, rows, width = tokens.shape
    top = expert_ids.shape[2]
    ep = lax.axis_size("ep")
    tp = lax.axis_size("tp")
    chips = tp // 2
    part = width // tp
    capacity = rows * top * 5 // (4 * ep)
    few = ep <= 8
    own_slot = lax.axis_index("ep")
    own_chip = lax.axis_index("tp") // 2
    own_core = lax.axis_index("tp") % 2
    slot_range = jnp.arange(ep, dtype=jnp.int32)
    chip_range = jnp.arange(chips, dtype=jnp.int32)
    core = jnp.full((chips,), own_core, jnp.int32)
    chip_order = (own_chip + chip_range) % chips
    columns = jnp.stack(
        [chip_range * 2 + 1 - own_core, chip_order, chip_order * 2 + own_core]
    )

    def along_ep(value, shift):
        return lax.ppermute(value, "ep", [(i, (i + shift) % ep) for i in range(ep)])

    def along_chips(value, shift):
        pairs = [
            (x * 2 + c, (x + shift) % chips * 2 + c) for x in range(chips) for c in range(2)
        ]
        return lax.ppermute(value, "tp", pairs)

    def along_cores(value):
        return lax.ppermute(value, "tp", [(i, i ^ 1) for i in range(tp)])

    def exchange(pieces, back):
        sign = -1 if back else 1
        if few:
            return [along_ep(piece, sign * (at + 1)) for at, piece in enumerate(pieces)]
        stacked = jnp.stack([pieces[0]] + pieces)
        placed = stacked[sign * (slot_range - own_slot) % ep]
        came = lax.all_to_all(placed, "ep", 0, 0, tiled=True)
        return list(came[(own_slot - sign * slot_range[1:]) % ep])

    weights = pltpu.with_memory_space_constraint(expert_weights, pltpu.HBM)
    arrived = {}
    for span in range(1, spans):
        sent = take(core, pltpu.with_memory_space_constraint(tokens, pltpu.HBM), span)
        arrived[span] = (tokens[span], exchange([sent] * (ep - 1), False))

    slot, rank, kept_gates, kept = routes(
        placement, slot_limit, expert_ids, replica_pick, gate_weights
    )
    place = (slot[0] - own_slot) % ep * capacity + rank[0]
    place = jnp.where(kept[0], place, ep * capacity)
    hits = place[:, :, None] == jnp.arange(ep * capacity, dtype=jnp.int32)
    choose = jnp.any(hits, axis=1).astype(jnp.bfloat16).T
    up_weights, down_weights, for_other = load(columns, weights)
    other_down = along_cores(for_other)
    own, others = pack(core, choose, tokens[0], ep)
    others, other_down = lax.optimization_barrier((others, other_down))
    arrived[0] = (own, exchange(others, False))

    def finish(span, after):
        own, pieces = arrived[span]
        if after is not None:
            own, after = lax.optimization_barrier((own, after))
        hidden = up(core, own, pieces, [along_cores(piece) for piece in pieces], up_weights)
        sums = down(columns, hidden, along_cores(hidden), down_weights, other_down)
        came = [along_chips(sums[shift], shift) for shift in range(1, chips)]
        totals = []
        count = own.shape[0]
        for piece in range(ep):
            at = slice(piece * count, (piece + 1) * count)
            total = sums[0][at].astype(jnp.float32)
            for value in came:
                total = total + value[at].astype(jnp.float32)
            totals.append(total.astype(jnp.bfloat16))
        return [totals[0]] + exchange(totals[1:], True), hidden

    returned = {}
    hidden = None
    for span in list(range(1, spans)) + [0]:
        returned[span], hidden = finish(span, hidden)

    old_table = placement[0]
    outs = []
    for span in range(spans):
        if span == 0:
            weight = jnp.sum(jnp.where(hits, kept_gates[0][:, :, None], 0.0), axis=1)
            outs.append(unpack(weight, returned[0]))
            continue
        serves = placement[span][:, None] == old_table[None, :]
        serving = jnp.min(jnp.where(serves, slot_range, ep), axis=1)
        served = jnp.sum(
            jnp.where(slot[span][:, :, None] == slot_range, (serving - own_slot) % ep, 0), axis=2
        )
        combined = jnp.zeros((rows, part), jnp.float32)
        for at in range(ep):
            share = jnp.sum(jnp.where(served == at, kept_gates[span], 0.0), axis=1)[:, None]
            value = share * returned[span][at].astype(jnp.float32)
            combined = combined + jnp.where(share != 0, value, 0.0)
        outs.append(combined.astype(jnp.bfloat16))
    return jnp.stack(outs)


def solution(mesh):
    placed = (
        P(None, ("groups", "ep"), None),
        P(None, ("groups", "ep"), None),
        P(None, ("groups", "ep"), None),
        P(None, ("groups", "ep"), None),
        P(),
        P(),
        P("ep", None, "tp", None),
    )
    return jax.shard_map(
        per_device,
        mesh=mesh,
        in_specs=placed,
        out_specs=P(None, ("groups", "ep"), "tp"),
        check_vma=False,
    )
```

```python
import functools

import jax
import jax.numpy as jnp
from jax import lax
from jax.experimental import pallas as pl
from jax.experimental.pallas import tpu as pltpu
from jax.sharding import PartitionSpec as P

VMEM_LIMIT = 32 * 1024 * 1024
CONTRACT_LAST = (((1,), (1,)), ((), ()))


def routes(placement, limits, chosen_ids, pick_values, gates):
    spans, rows, top = chosen_ids.shape
    slots = placement.shape[1]
    slot_range = jnp.arange(slots, dtype=jnp.int32)
    same = placement[:, :, None] == placement[:, None, :]
    before = slot_range[None, :] < slot_range[:, None]
    turn = jnp.sum((same & before).astype(jnp.int32), axis=2)
    flat_ids = chosen_ids.reshape(spans, rows * top)
    holders = flat_ids[:, :, None] == placement[:, None, :]
    count = jnp.sum(holders.astype(jnp.int32), axis=2)
    wanted = pick_values.reshape(spans, rows * top) % count
    onehot = holders & (turn[:, None, :] == wanted[:, :, None])
    slot = jnp.sum(jnp.where(onehot, slot_range, 0), axis=2)
    limit = jnp.sum(jnp.where(onehot, limits, 0), axis=2)
    order = jnp.arange(rows * top, dtype=jnp.int32)
    ahead = (slot[:, :, None] == slot[:, None, :]) & (order[None, :] < order[:, None])
    rank = jnp.sum(ahead.astype(jnp.int32), axis=2)
    kept = rank < limit
    shape = (spans, rows, top)
    return (
        slot.reshape(shape),
        rank.reshape(shape),
        jnp.where(kept.reshape(shape), gates, 0.0),
        kept.reshape(shape),
    )


def in_vmem(count):
    return [pl.BlockSpec(memory_space=pltpu.VMEM)] * count


def with_core(count):
    return [pl.BlockSpec(memory_space=pltpu.SMEM)] + in_vmem(count)


def params():
    return pltpu.CompilerParams(vmem_limit_bytes=VMEM_LIMIT)


def cost(rows, width, units):
    return pl.CostEstimate(flops=2 * rows, bytes_accessed=2 * rows, transcendentals=0)


def in_hbm():
    return pl.BlockSpec(memory_space=pltpu.HBM)


def take_kernel(lead, side, core_ref, from_ref, out_ref, sems):
    chips = core_ref.shape[0]
    part = from_ref.shape[-1] // (2 * chips)
    copies = []
    for chip in range(chips):
        core = core_ref[chip] if side == 0 else 1 - core_ref[chip]
        at = pl.multiple_of((2 * chip + core) * part, part)
        if len(out_ref.shape) == 3:
            to = out_ref.at[chip]
        else:
            to = out_ref.at[:, chip * part : (chip + 1) * part]
        copies.append(
            pltpu.make_async_copy(from_ref.at[*lead, :, pl.ds(at, part)], to, sems.at[chip])
        )
    for copy in copies:
        copy.start()
    for copy in copies:
        copy.wait()


def take(core, values, lead, side, stacked):
    chips = core.shape[0]
    rows, width = values.shape[-2:]
    part = width // (2 * chips)
    shape = (chips, rows, part) if stacked else (rows, chips * part)
    return pl.pallas_call(
        functools.partial(take_kernel, lead, side),
        out_shape=jax.ShapeDtypeStruct(shape, jnp.bfloat16),
        in_specs=[pl.BlockSpec(memory_space=pltpu.SMEM), in_hbm()],
        out_specs=in_vmem(1)[0],
        scratch_shapes=[pltpu.SemaphoreType.DMA((chips,))],
        compiler_params=params(),
        cost_estimate=cost(rows, width, 1),
    )(core, values)


def pack_kernel(core_ref, choose_ref, rows_ref, own_ref, *out_refs):
    chips = core_ref.shape[0]
    count = own_ref.shape[0]
    part = own_ref.shape[1] // (2 * chips)
    first = core_ref[0] == 0
    choose = choose_ref[...]
    for chip in range(chips):
        of = 2 * chip * part
        low = jnp.dot(
            choose, rows_ref[:, of : of + part], preferred_element_type=jnp.float32
        )
        high = jnp.dot(
            choose, rows_ref[:, of + part : of + 2 * part], preferred_element_type=jnp.float32
        )
        own_ref[:, of : of + part] = low[:count].astype(jnp.bfloat16)
        own_ref[:, of + part : of + 2 * part] = high[:count].astype(jnp.bfloat16)
        sent = jnp.where(first, low, high)
        for index, out_ref in enumerate(out_refs):
            at = (index + 1) * count
            out_ref[:, chip * part : (chip + 1) * part] = sent[at : at + count].astype(jnp.bfloat16)


def pack(core, choose, rows, slots):
    count = choose.shape[0] // slots
    width = rows.shape[1]
    outs = [jax.ShapeDtypeStruct((count, width), jnp.bfloat16)]
    outs += [jax.ShapeDtypeStruct((count, width // 2), jnp.bfloat16)] * (slots - 1)
    own, *others = pl.pallas_call(
        pack_kernel,
        out_shape=outs,
        in_specs=with_core(2),
        out_specs=in_vmem(slots),
        compiler_params=params(),
        cost_estimate=cost(choose.shape[0], choose.shape[1], width),
    )(core, choose, rows)
    return own, others


def load_kernel(columns_ref, from_ref, up_ref, down_ref, sems):
    parts = up_ref.shape[0]
    chips = down_ref.shape[0]
    part = up_ref.shape[3]
    copies = []
    for index in range(parts):
        copies.append(
            pltpu.make_async_copy(
                from_ref.at[0, 0:2, :, index * part : (index + 1) * part],
                up_ref.at[index],
                sems.at[index],
            )
        )
    for chip in range(chips):
        at = pl.multiple_of(columns_ref[0, chip] * part, part)
        copies.append(
            pltpu.make_async_copy(
                from_ref.at[0, 2, :, pl.ds(at, part)], down_ref.at[chip], sems.at[parts + chip]
            )
        )
    for copy in copies:
        copy.start()
    for copy in copies:
        copy.wait()


def load(columns, weights):
    chips = columns.shape[1]
    units, width = weights.shape[2:]
    part = width // (2 * chips)
    return pl.pallas_call(
        load_kernel,
        out_shape=[
            pltpu.VMEM((2 * chips, 2, units, part), jnp.bfloat16),
            pltpu.VMEM((chips, units, part), jnp.bfloat16),
        ],
        in_specs=[pl.BlockSpec(memory_space=pltpu.SMEM), in_hbm()],
        out_specs=in_vmem(2),
        scratch_shapes=[pltpu.SemaphoreType.DMA((3 * chips,))],
        compiler_params=params(),
        cost_estimate=cost(3 * units, width, 1),
    )(columns, weights)


def up_kernel(core_ref, own_ref, *refs):
    *piece_refs, weight_ref, hidden_ref, rows_ref = refs
    chips = core_ref.shape[0]
    count = len(piece_refs) // 2
    part = own_ref.shape[1] // (2 * chips)
    first = core_ref[0] == 0
    gate = upward = 0.0
    for index in range(2 * chips):
        chip, core = index // 2, index % 2
        column = slice(index * part, (index + 1) * part)
        of = slice(chip * part, (chip + 1) * part)
        values = [own_ref[:, column]]
        for piece in range(count):
            own, other = piece_refs[piece][:, of], piece_refs[count + piece][:, of]
            values.append(
                jnp.where(first, own, other) if core == 0 else jnp.where(first, other, own)
            )
        if all(value.shape[0] % 16 == 0 for value in values):
            at = 0
            for value in values:
                rows_ref[at : at + value.shape[0]] = value
                at += value.shape[0]
        else:
            joined = jnp.concatenate([value.astype(jnp.float32) for value in values])
            rows_ref[...] = joined.astype(jnp.bfloat16)
        rows = rows_ref[...]
        gate += lax.dot_general(
            rows, weight_ref[index, 0], CONTRACT_LAST, preferred_element_type=jnp.float32
        )
        upward += lax.dot_general(
            rows, weight_ref[index, 1], CONTRACT_LAST, preferred_element_type=jnp.float32
        )
    hidden_ref[...] = (gate / (1.0 + jnp.exp(-gate)) * upward).astype(jnp.bfloat16)


def up(core, own, own_pieces, other_pieces, weights):
    total, width = own.shape[0] + sum(piece.shape[0] for piece in own_pieces), own.shape[1]
    units, part = weights.shape[2:]
    return pl.pallas_call(
        up_kernel,
        out_shape=jax.ShapeDtypeStruct((total, units), jnp.bfloat16),
        in_specs=with_core(2 * len(own_pieces) + 2),
        out_specs=in_vmem(1)[0],
        scratch_shapes=[pltpu.VMEM((total, part), jnp.bfloat16)],
        compiler_params=params(),
        cost_estimate=cost(total, width, 2 * units),
    )(core, own, *own_pieces, *other_pieces, weights)


def down_kernel(columns_ref, hidden_ref, other_hidden_ref, weight_ref, other_ref, *out_refs):
    hidden, other_hidden = hidden_ref[...], other_hidden_ref[...]
    for shift, out_ref in enumerate(out_refs):
        total = jnp.dot(hidden, weight_ref[shift], preferred_element_type=jnp.float32)
        total += jnp.dot(
            other_hidden, other_ref[columns_ref[1, shift]], preferred_element_type=jnp.float32
        )
        out_ref[...] = total.astype(jnp.bfloat16)


def down(columns, hidden, other_hidden, weights, other_weights):
    chips, units, part = other_weights.shape
    rows = hidden.shape[0]
    return pl.pallas_call(
        down_kernel,
        out_shape=[jax.ShapeDtypeStruct((rows, part), jnp.bfloat16)] * chips,
        in_specs=with_core(4),
        out_specs=in_vmem(chips),
        compiler_params=params(),
        cost_estimate=cost(rows, 2 * units, chips * part),
    )(columns, hidden, other_hidden, weights, other_weights)


def unpack_kernel(weight_ref, *refs):
    *piece_refs, out_ref = refs
    rows = jnp.concatenate([ref[...].astype(jnp.float32) for ref in piece_refs])
    rows = rows.astype(jnp.bfloat16)
    weight = weight_ref[...]
    high = weight.astype(jnp.bfloat16)
    low = (weight - high.astype(jnp.float32)).astype(jnp.bfloat16)
    total = jnp.dot(high, rows, preferred_element_type=jnp.float32)
    total += jnp.dot(low, rows, preferred_element_type=jnp.float32)
    out_ref[...] = total.astype(jnp.bfloat16)


def unpack(weight, pieces):
    rows, part = weight.shape[0], pieces[0].shape[1]
    return pl.pallas_call(
        unpack_kernel,
        out_shape=jax.ShapeDtypeStruct((rows, part), jnp.bfloat16),
        in_specs=in_vmem(1 + len(pieces)),
        out_specs=in_vmem(1)[0],
        compiler_params=params(),
        cost_estimate=cost(rows, weight.shape[1], part),
    )(weight, *pieces)


def per_device(
    tokens, expert_ids, gate_weights, replica_pick, placement, slot_limit, expert_weights
):
    spans, rows, width = tokens.shape
    top = expert_ids.shape[2]
    ep = lax.axis_size("ep")
    tp = lax.axis_size("tp")
    chips = tp // 2
    part = width // tp
    capacity = rows * top * 5 // (4 * ep)
    few = ep <= 8
    own_slot = lax.axis_index("ep")
    own_chip = lax.axis_index("tp") // 2
    own_core = lax.axis_index("tp") % 2
    slot_range = jnp.arange(ep, dtype=jnp.int32)
    chip_range = jnp.arange(chips, dtype=jnp.int32)
    core = jnp.full((chips,), own_core, jnp.int32)
    chip_order = (own_chip + chip_range) % chips
    columns = jnp.stack([chip_order * 2 + own_core, chip_order])

    def along_ep(value, shift):
        return lax.ppermute(value, "ep", [(i, (i + shift) % ep) for i in range(ep)])

    def along_chips(value, shift):
        pairs = [
            (x * 2 + c, (x + shift) % chips * 2 + c) for x in range(chips) for c in range(2)
        ]
        return lax.ppermute(value, "tp", pairs)

    def along_cores(value):
        return lax.ppermute(value, "tp", [(i, i ^ 1) for i in range(tp)])

    def exchange(pieces, back):
        sign = -1 if back else 1
        if few:
            return [along_ep(piece, sign * (at + 1)) for at, piece in enumerate(pieces)]
        stacked = jnp.stack([pieces[0]] + pieces)
        placed = stacked[sign * (slot_range - own_slot) % ep]
        came = lax.all_to_all(placed, "ep", 0, 0, tiled=True)
        return list(came[(own_slot - sign * slot_range[1:]) % ep])

    weights = pltpu.with_memory_space_constraint(expert_weights, pltpu.HBM)
    arrived = {}
    for span in range(1, spans):
        sent = take(core, pltpu.with_memory_space_constraint(tokens, pltpu.HBM), (span,), 0, False)
        arrived[span] = (tokens[span], exchange([sent] * (ep - 1), False))

    slot, rank, kept_gates, kept = routes(
        placement, slot_limit, expert_ids, replica_pick, gate_weights
    )
    place = (slot[0] - own_slot) % ep * capacity + rank[0]
    place = jnp.where(kept[0], place, ep * capacity)
    hits = place[:, :, None] == jnp.arange(ep * capacity, dtype=jnp.int32)
    choose = jnp.any(hits, axis=1).astype(jnp.bfloat16).T
    own, others = pack(core, choose, tokens[0], ep)
    for_other = take(core, weights, (0, 2), 1, True)
    for_other, others = lax.optimization_barrier((for_other, others))
    other_down = along_cores(for_other)
    last_own, last = arrived[spans - 1]
    weights, last[0] = lax.optimization_barrier((weights, last[0]))
    up_weights, down_weights = load(
        columns, pltpu.with_memory_space_constraint(weights, pltpu.HBM)
    )

    swapped = {}
    for span in range(1, spans):
        own_rows, pieces = arrived[span]
        both = (pieces, [along_cores(piece) for piece in pieces])
        both, others, other_down = lax.optimization_barrier((both, others, other_down))
        arrived[span], swapped[span] = (own_rows, both[0]), both[1]
    arrived[0] = (own, exchange(others, False))

    def finish(span, after):
        own, pieces = arrived[span]
        if after is not None:
            own, pieces, after = lax.optimization_barrier((own, pieces, after))
        others = swapped.get(span) or [along_cores(piece) for piece in pieces]
        hidden = up(core, own, pieces, others, up_weights)
        sums = down(columns, hidden, along_cores(hidden), down_weights, other_down)
        came = [along_chips(sums[shift], shift) for shift in range(1, chips)]
        totals = []
        count = own.shape[0]
        for piece in range(ep):
            at = slice(piece * count, (piece + 1) * count)
            total = sums[0][at].astype(jnp.float32)
            for value in came:
                total = total + value[at].astype(jnp.float32)
            totals.append(total.astype(jnp.bfloat16))
        return [totals[0]] + exchange(totals[1:], True), sums

    returned = {}
    hidden = None
    for span in list(range(1, spans)) + [0]:
        returned[span], hidden = finish(span, hidden)

    old_table = placement[0]
    outs = []
    for span in range(spans):
        if span == 0:
            weight = jnp.sum(jnp.where(hits, kept_gates[0][:, :, None], 0.0), axis=1)
            outs.append(unpack(weight, returned[0]))
            continue
        serves = placement[span][:, None] == old_table[None, :]
        serving = jnp.min(jnp.where(serves, slot_range, ep), axis=1)
        served = jnp.sum(
            jnp.where(slot[span][:, :, None] == slot_range, (serving - own_slot) % ep, 0), axis=2
        )
        combined = jnp.zeros((rows, part), jnp.float32)
        for at in range(ep):
            share = jnp.sum(jnp.where(served == at, kept_gates[span], 0.0), axis=1)[:, None]
            value = share * returned[span][at].astype(jnp.float32)
            combined = combined + jnp.where(share != 0, value, 0.0)
        outs.append(combined.astype(jnp.bfloat16))
    return jnp.stack(outs)


def solution(mesh):
    placed = (
        P(None, ("groups", "ep"), None),
        P(None, ("groups", "ep"), None),
        P(None, ("groups", "ep"), None),
        P(None, ("groups", "ep"), None),
        P(),
        P(),
        P("ep", None, "tp", None),
    )
    return jax.shard_map(
        per_device,
        mesh=mesh,
        in_specs=placed,
        out_specs=P(None, ("groups", "ep"), "tp"),
        check_vma=False,
    )
```

```python
import functools

import jax
import jax.numpy as jnp
from jax import lax
from jax.experimental import pallas as pl
from jax.experimental.pallas import tpu as pltpu
from jax.sharding import PartitionSpec as P

VMEM_LIMIT = 32 * 1024 * 1024
CONTRACT_LAST = (((1,), (1,)), ((), ()))


def routes(placement, limits, chosen_ids, pick_values, gates):
    spans, rows, top = chosen_ids.shape
    slots = placement.shape[1]
    slot_range = jnp.arange(slots, dtype=jnp.int32)
    same = placement[:, :, None] == placement[:, None, :]
    before = slot_range[None, :] < slot_range[:, None]
    turn = jnp.sum((same & before).astype(jnp.int32), axis=2)
    flat_ids = chosen_ids.reshape(spans, rows * top)
    holders = flat_ids[:, :, None] == placement[:, None, :]
    count = jnp.sum(holders.astype(jnp.int32), axis=2)
    wanted = pick_values.reshape(spans, rows * top) % count
    onehot = holders & (turn[:, None, :] == wanted[:, :, None])
    slot = jnp.sum(jnp.where(onehot, slot_range, 0), axis=2)
    limit = jnp.sum(jnp.where(onehot, limits, 0), axis=2)
    order = jnp.arange(rows * top, dtype=jnp.int32)
    ahead = (slot[:, :, None] == slot[:, None, :]) & (order[None, :] < order[:, None])
    rank = jnp.sum(ahead.astype(jnp.int32), axis=2)
    kept = rank < limit
    shape = (spans, rows, top)
    return (
        slot.reshape(shape),
        rank.reshape(shape),
        jnp.where(kept.reshape(shape), gates, 0.0),
        kept.reshape(shape),
    )


def in_vmem(count):
    return [pl.BlockSpec(memory_space=pltpu.VMEM)] * count


def with_core(count):
    return [pl.BlockSpec(memory_space=pltpu.SMEM)] + in_vmem(count)


def params():
    return pltpu.CompilerParams(vmem_limit_bytes=VMEM_LIMIT)


def cost(rows, width, units):
    return pl.CostEstimate(flops=2 * rows, bytes_accessed=2 * rows, transcendentals=0)


def in_hbm():
    return pl.BlockSpec(memory_space=pltpu.HBM)


def take_kernel(lead, side, core_ref, from_ref, out_ref, sems):
    chips = core_ref.shape[0]
    part = from_ref.shape[-1] // (2 * chips)
    copies = []
    for chip in range(chips):
        core = core_ref[chip] if side == 0 else 1 - core_ref[chip]
        at = pl.multiple_of((2 * chip + core) * part, part)
        if len(out_ref.shape) == 3:
            to = out_ref.at[chip]
        else:
            to = out_ref.at[:, chip * part : (chip + 1) * part]
        copies.append(
            pltpu.make_async_copy(from_ref.at[*lead, :, pl.ds(at, part)], to, sems.at[chip])
        )
    for copy in copies:
        copy.start()
    for copy in copies:
        copy.wait()


def take(core, values, lead, side, stacked):
    chips = core.shape[0]
    rows, width = values.shape[-2:]
    part = width // (2 * chips)
    shape = (chips, rows, part) if stacked else (rows, chips * part)
    return pl.pallas_call(
        functools.partial(take_kernel, lead, side),
        out_shape=jax.ShapeDtypeStruct(shape, jnp.bfloat16),
        in_specs=[pl.BlockSpec(memory_space=pltpu.SMEM), in_hbm()],
        out_specs=in_vmem(1)[0],
        scratch_shapes=[pltpu.SemaphoreType.DMA((chips,))],
        compiler_params=params(),
        cost_estimate=cost(rows, width, 1),
    )(core, values)


def pack_kernel(core_ref, choose_ref, rows_ref, own_ref, *out_refs):
    chips = core_ref.shape[0]
    count = own_ref.shape[0]
    part = own_ref.shape[1] // (2 * chips)
    first = core_ref[0] == 0
    choose = choose_ref[...]
    for chip in range(chips):
        of = 2 * chip * part
        low = jnp.dot(
            choose, rows_ref[:, of : of + part], preferred_element_type=jnp.float32
        )
        high = jnp.dot(
            choose, rows_ref[:, of + part : of + 2 * part], preferred_element_type=jnp.float32
        )
        own_ref[:, of : of + part] = low[:count].astype(jnp.bfloat16)
        own_ref[:, of + part : of + 2 * part] = high[:count].astype(jnp.bfloat16)
        sent = jnp.where(first, low, high)
        for index, out_ref in enumerate(out_refs):
            at = (index + 1) * count
            out_ref[:, chip * part : (chip + 1) * part] = sent[at : at + count].astype(jnp.bfloat16)


def pack(core, choose, rows, slots):
    count = choose.shape[0] // slots
    width = rows.shape[1]
    outs = [jax.ShapeDtypeStruct((count, width), jnp.bfloat16)]
    outs += [jax.ShapeDtypeStruct((count, width // 2), jnp.bfloat16)] * (slots - 1)
    own, *others = pl.pallas_call(
        pack_kernel,
        out_shape=outs,
        in_specs=with_core(2),
        out_specs=in_vmem(slots),
        compiler_params=params(),
        cost_estimate=cost(choose.shape[0], choose.shape[1], width),
    )(core, choose, rows)
    return own, others


def project(core_ref, own_ref, piece_refs, weight_ref, hidden_ref, rows_ref, before):
    chips = core_ref.shape[0]
    count = len(piece_refs) // 2
    part = own_ref.shape[1] // (2 * chips)
    first = core_ref[0] == 0
    gate = upward = 0.0
    for index in range(2 * chips):
        chip, core = index // 2, index % 2
        column = slice(index * part, (index + 1) * part)
        of = slice(chip * part, (chip + 1) * part)
        values = [own_ref[:, column]]
        for piece in range(count):
            own, other = piece_refs[piece][:, of], piece_refs[count + piece][:, of]
            values.append(
                jnp.where(first, own, other) if core == 0 else jnp.where(first, other, own)
            )
        if all(value.shape[0] % 16 == 0 for value in values):
            at = 0
            for value in values:
                rows_ref[at : at + value.shape[0]] = value
                at += value.shape[0]
        else:
            joined = jnp.concatenate([value.astype(jnp.float32) for value in values])
            rows_ref[...] = joined.astype(jnp.bfloat16)
        rows = rows_ref[...]
        before(index)
        gate += lax.dot_general(
            rows, weight_ref[index, 0], CONTRACT_LAST, preferred_element_type=jnp.float32
        )
        upward += lax.dot_general(
            rows, weight_ref[index, 1], CONTRACT_LAST, preferred_element_type=jnp.float32
        )
    hidden_ref[...] = (gate / (1.0 + jnp.exp(-gate)) * upward).astype(jnp.bfloat16)


def up_kernel(core_ref, own_ref, *refs):
    *piece_refs, weight_ref, hidden_ref, rows_ref = refs
    project(core_ref, own_ref, piece_refs, weight_ref, hidden_ref, rows_ref, lambda index: None)


def first_up_kernel(core_ref, columns_ref, own_ref, *refs):
    *piece_refs, from_ref, hidden_ref, weight_ref, down_ref, rows_ref, sems = refs
    parts = weight_ref.shape[0]
    chips = down_ref.shape[0]
    part = weight_ref.shape[3]
    copies = [
        pltpu.make_async_copy(
            from_ref.at[0, 0:2, :, index * part : (index + 1) * part],
            weight_ref.at[index],
            sems.at[index],
        )
        for index in range(parts)
    ]
    for chip in range(chips):
        at = pl.multiple_of(columns_ref[0, chip] * part, part)
        copies.append(
            pltpu.make_async_copy(
                from_ref.at[0, 2, :, pl.ds(at, part)], down_ref.at[chip], sems.at[parts + chip]
            )
        )
    ahead = 3
    for copy in copies[:ahead]:
        copy.start()

    def before(index):
        copies[index].wait()
        if index + ahead < len(copies):
            copies[index + ahead].start()

    project(core_ref, own_ref, piece_refs, weight_ref, hidden_ref, rows_ref, before)
    for index in range(parts, len(copies)):
        before(index)


def first_up(core, columns, own, own_pieces, other_pieces, weights):
    chips = core.shape[0]
    total = own.shape[0] + sum(piece.shape[0] for piece in own_pieces)
    units, width = weights.shape[2:]
    part = width // (2 * chips)
    return pl.pallas_call(
        first_up_kernel,
        out_shape=[
            jax.ShapeDtypeStruct((total, units), jnp.bfloat16),
            pltpu.VMEM((2 * chips, 2, units, part), jnp.bfloat16),
            pltpu.VMEM((chips, units, part), jnp.bfloat16),
        ],
        in_specs=[pl.BlockSpec(memory_space=pltpu.SMEM)] * 2
        + in_vmem(2 * len(own_pieces) + 1)
        + [in_hbm()],
        out_specs=in_vmem(3),
        scratch_shapes=[
            pltpu.VMEM((total, part), jnp.bfloat16),
            pltpu.SemaphoreType.DMA((3 * chips,)),
        ],
        compiler_params=params(),
        cost_estimate=cost(total, width, 2 * units),
    )(core, columns, own, *own_pieces, *other_pieces, weights)


def up(core, own, own_pieces, other_pieces, weights):
    total, width = own.shape[0] + sum(piece.shape[0] for piece in own_pieces), own.shape[1]
    units, part = weights.shape[2:]
    return pl.pallas_call(
        up_kernel,
        out_shape=jax.ShapeDtypeStruct((total, units), jnp.bfloat16),
        in_specs=with_core(2 * len(own_pieces) + 2),
        out_specs=in_vmem(1)[0],
        scratch_shapes=[pltpu.VMEM((total, part), jnp.bfloat16)],
        compiler_params=params(),
        cost_estimate=cost(total, width, 2 * units),
    )(core, own, *own_pieces, *other_pieces, weights)


def down_kernel(columns_ref, hidden_ref, other_hidden_ref, weight_ref, other_ref, *out_refs):
    hidden, other_hidden = hidden_ref[...], other_hidden_ref[...]
    for shift, out_ref in enumerate(out_refs):
        total = jnp.dot(hidden, weight_ref[shift], preferred_element_type=jnp.float32)
        total += jnp.dot(
            other_hidden, other_ref[columns_ref[1, shift]], preferred_element_type=jnp.float32
        )
        out_ref[...] = total.astype(jnp.bfloat16)


def down(columns, hidden, other_hidden, weights, other_weights):
    chips, units, part = other_weights.shape
    rows = hidden.shape[0]
    return pl.pallas_call(
        down_kernel,
        out_shape=[jax.ShapeDtypeStruct((rows, part), jnp.bfloat16)] * chips,
        in_specs=with_core(4),
        out_specs=in_vmem(chips),
        compiler_params=params(),
        cost_estimate=cost(rows, 2 * units, chips * part),
    )(columns, hidden, other_hidden, weights, other_weights)


def unpack_kernel(weight_ref, *refs):
    *piece_refs, out_ref = refs
    rows = jnp.concatenate([ref[...].astype(jnp.float32) for ref in piece_refs])
    rows = rows.astype(jnp.bfloat16)
    weight = weight_ref[...]
    high = weight.astype(jnp.bfloat16)
    low = (weight - high.astype(jnp.float32)).astype(jnp.bfloat16)
    total = jnp.dot(high, rows, preferred_element_type=jnp.float32)
    total += jnp.dot(low, rows, preferred_element_type=jnp.float32)
    out_ref[...] = total.astype(jnp.bfloat16)


def unpack(weight, pieces):
    rows, part = weight.shape[0], pieces[0].shape[1]
    return pl.pallas_call(
        unpack_kernel,
        out_shape=jax.ShapeDtypeStruct((rows, part), jnp.bfloat16),
        in_specs=in_vmem(1 + len(pieces)),
        out_specs=in_vmem(1)[0],
        compiler_params=params(),
        cost_estimate=cost(rows, weight.shape[1], part),
    )(weight, *pieces)


def per_device(
    tokens, expert_ids, gate_weights, replica_pick, placement, slot_limit, expert_weights
):
    spans, rows, width = tokens.shape
    top = expert_ids.shape[2]
    ep = lax.axis_size("ep")
    tp = lax.axis_size("tp")
    chips = tp // 2
    part = width // tp
    capacity = rows * top * 5 // (4 * ep)
    few = ep <= 8
    own_slot = lax.axis_index("ep")
    own_chip = lax.axis_index("tp") // 2
    own_core = lax.axis_index("tp") % 2
    slot_range = jnp.arange(ep, dtype=jnp.int32)
    chip_range = jnp.arange(chips, dtype=jnp.int32)
    core = jnp.full((chips,), own_core, jnp.int32)
    chip_order = (own_chip + chip_range) % chips
    columns = jnp.stack([chip_order * 2 + own_core, chip_order])

    def along_ep(value, shift):
        return lax.ppermute(value, "ep", [(i, (i + shift) % ep) for i in range(ep)])

    def along_chips(value, shift):
        pairs = [
            (x * 2 + c, (x + shift) % chips * 2 + c) for x in range(chips) for c in range(2)
        ]
        return lax.ppermute(value, "tp", pairs)

    def along_cores(value):
        return lax.ppermute(value, "tp", [(i, i ^ 1) for i in range(tp)])

    def exchange(pieces, back):
        sign = -1 if back else 1
        if few:
            return [along_ep(piece, sign * (at + 1)) for at, piece in enumerate(pieces)]
        stacked = jnp.stack([pieces[0]] + pieces)
        placed = stacked[sign * (slot_range - own_slot) % ep]
        came = lax.all_to_all(placed, "ep", 0, 0, tiled=True)
        return list(came[(own_slot - sign * slot_range[1:]) % ep])

    weights = pltpu.with_memory_space_constraint(expert_weights, pltpu.HBM)
    arrived = {}
    for span in range(1, spans):
        sent = take(core, pltpu.with_memory_space_constraint(tokens, pltpu.HBM), (span,), 0, False)
        arrived[span] = (tokens[span], exchange([sent] * (ep - 1), False))

    slot, rank, kept_gates, kept = routes(
        placement, slot_limit, expert_ids, replica_pick, gate_weights
    )
    place = (slot[0] - own_slot) % ep * capacity + rank[0]
    place = jnp.where(kept[0], place, ep * capacity)
    hits = place[:, :, None] == jnp.arange(ep * capacity, dtype=jnp.int32)
    choose = jnp.any(hits, axis=1).astype(jnp.bfloat16).T
    own, others = pack(core, choose, tokens[0], ep)
    for_other = take(core, weights, (0, 2), 1, True)
    for_other, others = lax.optimization_barrier((for_other, others))
    other_down = along_cores(for_other)
    swapped = {}
    for span in range(1, spans):
        own_rows, pieces = arrived[span]
        both = (pieces, [along_cores(piece) for piece in pieces])
        same = core
        both, others, other_down, same, weights = lax.optimization_barrier(
            (both, others, other_down, same, weights)
        )
        arrived[span], swapped[span] = (own_rows, both[0]), both[1]
        same = along_chips(same, 1)
    arrived[0] = (own, exchange(others, False))

    kept_weights = []

    def finish(span, after):
        own, pieces = arrived[span]
        if after is not None:
            own, pieces, after = lax.optimization_barrier((own, pieces, after))
        others = swapped.get(span) or [along_cores(piece) for piece in pieces]
        if after is None:
            hidden, *loaded = first_up(
                core,
                columns,
                own,
                pieces,
                others,
                pltpu.with_memory_space_constraint(weights, pltpu.HBM),
            )
            kept_weights.extend(loaded)
            hidden, core_there = lax.optimization_barrier((hidden, same))
        else:
            hidden = up(after[1], own, pieces, others, kept_weights[0])
            core_there = core
        sums = down(columns, hidden, along_cores(hidden), kept_weights[1], other_down)
        came = [along_chips(sums[shift], shift) for shift in range(1, chips)]
        totals = []
        count = own.shape[0]
        for piece in range(ep):
            at = slice(piece * count, (piece + 1) * count)
            total = sums[0][at].astype(jnp.float32)
            for value in came:
                total = total + value[at].astype(jnp.float32)
            totals.append(total.astype(jnp.bfloat16))
        return [totals[0]] + exchange(totals[1:], True), (sums, core_there)

    returned = {}
    hidden = None
    for span in list(range(1, spans)) + [0]:
        returned[span], hidden = finish(span, hidden)

    old_table = placement[0]
    outs = []
    for span in range(spans):
        if span == 0:
            weight = jnp.sum(jnp.where(hits, kept_gates[0][:, :, None], 0.0), axis=1)
            outs.append(unpack(weight, returned[0]))
            continue
        serves = placement[span][:, None] == old_table[None, :]
        serving = jnp.min(jnp.where(serves, slot_range, ep), axis=1)
        served = jnp.sum(
            jnp.where(slot[span][:, :, None] == slot_range, (serving - own_slot) % ep, 0), axis=2
        )
        combined = jnp.zeros((rows, part), jnp.float32)
        for at in range(ep):
            share = jnp.sum(jnp.where(served == at, kept_gates[span], 0.0), axis=1)[:, None]
            value = share * returned[span][at].astype(jnp.float32)
            combined = combined + jnp.where(share != 0, value, 0.0)
        outs.append(combined.astype(jnp.bfloat16))
    return jnp.stack(outs)


def solution(mesh):
    placed = (
        P(None, ("groups", "ep"), None),
        P(None, ("groups", "ep"), None),
        P(None, ("groups", "ep"), None),
        P(None, ("groups", "ep"), None),
        P(),
        P(),
        P("ep", None, "tp", None),
    )
    return jax.shard_map(
        per_device,
        mesh=mesh,
        in_specs=placed,
        out_specs=P(None, ("groups", "ep"), "tp"),
        check_vma=False,
    )
```

```python
import functools

import jax
import jax.numpy as jnp
from jax import lax
from jax.experimental import pallas as pl
from jax.experimental.pallas import tpu as pltpu
from jax.sharding import PartitionSpec as P

VMEM_LIMIT = 32 * 1024 * 1024
CONTRACT_LAST = (((1,), (1,)), ((), ()))


def routes(placement, limits, chosen_ids, pick_values, gates):
    spans, rows, top = chosen_ids.shape
    slots = placement.shape[1]
    slot_range = jnp.arange(slots, dtype=jnp.int32)
    same = placement[:, :, None] == placement[:, None, :]
    before = slot_range[None, :] < slot_range[:, None]
    turn = jnp.sum((same & before).astype(jnp.int32), axis=2)
    flat_ids = chosen_ids.reshape(spans, rows * top)
    holders = flat_ids[:, :, None] == placement[:, None, :]
    count = jnp.sum(holders.astype(jnp.int32), axis=2)
    wanted = pick_values.reshape(spans, rows * top) % count
    onehot = holders & (turn[:, None, :] == wanted[:, :, None])
    slot = jnp.sum(jnp.where(onehot, slot_range, 0), axis=2)
    limit = jnp.sum(jnp.where(onehot, limits, 0), axis=2)
    order = jnp.arange(rows * top, dtype=jnp.int32)
    ahead = (slot[:, :, None] == slot[:, None, :]) & (order[None, :] < order[:, None])
    rank = jnp.sum(ahead.astype(jnp.int32), axis=2)
    kept = rank < limit
    shape = (spans, rows, top)
    return (
        slot.reshape(shape),
        rank.reshape(shape),
        jnp.where(kept.reshape(shape), gates, 0.0),
        kept.reshape(shape),
    )


def in_vmem(count):
    return [pl.BlockSpec(memory_space=pltpu.VMEM)] * count


def with_core(count):
    return [pl.BlockSpec(memory_space=pltpu.SMEM)] + in_vmem(count)


def params():
    return pltpu.CompilerParams(vmem_limit_bytes=VMEM_LIMIT)


def cost(rows, width, units):
    return pl.CostEstimate(flops=2 * rows, bytes_accessed=2 * rows, transcendentals=0)


def in_hbm():
    return pl.BlockSpec(memory_space=pltpu.HBM)


def take_kernel(lead, side, core_ref, from_ref, out_ref, sems):
    chips = core_ref.shape[0]
    part = from_ref.shape[-1] // (2 * chips)
    copies = []
    for chip in range(chips):
        core = core_ref[chip] if side == 0 else 1 - core_ref[chip]
        at = pl.multiple_of((2 * chip + core) * part, part)
        if len(out_ref.shape) == 3:
            to = out_ref.at[chip]
        else:
            to = out_ref.at[:, chip * part : (chip + 1) * part]
        copies.append(
            pltpu.make_async_copy(from_ref.at[*lead, :, pl.ds(at, part)], to, sems.at[chip])
        )
    for copy in copies:
        copy.start()
    for copy in copies:
        copy.wait()


def take(core, values, lead, side, stacked):
    chips = core.shape[0]
    rows, width = values.shape[-2:]
    part = width // (2 * chips)
    shape = (chips, rows, part) if stacked else (rows, chips * part)
    return pl.pallas_call(
        functools.partial(take_kernel, lead, side),
        out_shape=jax.ShapeDtypeStruct(shape, jnp.bfloat16),
        in_specs=[pl.BlockSpec(memory_space=pltpu.SMEM), in_hbm()],
        out_specs=in_vmem(1)[0],
        scratch_shapes=[pltpu.SemaphoreType.DMA((chips,))],
        compiler_params=params(),
        cost_estimate=cost(rows, width, 1),
    )(core, values)


def pack_kernel(core_ref, choose_ref, rows_ref, own_ref, *out_refs):
    chips = core_ref.shape[0]
    count = own_ref.shape[0]
    part = own_ref.shape[1] // (2 * chips)
    first = core_ref[0] == 0
    choose = choose_ref[...]
    for chip in range(chips):
        of = 2 * chip * part
        low = jnp.dot(
            choose, rows_ref[:, of : of + part], preferred_element_type=jnp.float32
        )
        high = jnp.dot(
            choose, rows_ref[:, of + part : of + 2 * part], preferred_element_type=jnp.float32
        )
        own_ref[:, of : of + part] = low[:count].astype(jnp.bfloat16)
        own_ref[:, of + part : of + 2 * part] = high[:count].astype(jnp.bfloat16)
        sent = jnp.where(first, low, high)
        for index, out_ref in enumerate(out_refs):
            at = (index + 1) * count
            out_ref[:, chip * part : (chip + 1) * part] = sent[at : at + count].astype(jnp.bfloat16)


def pack(core, choose, rows, slots):
    count = choose.shape[0] // slots
    width = rows.shape[1]
    outs = [jax.ShapeDtypeStruct((count, width), jnp.bfloat16)]
    outs += [jax.ShapeDtypeStruct((count, width // 2), jnp.bfloat16)] * (slots - 1)
    own, *others = pl.pallas_call(
        pack_kernel,
        out_shape=outs,
        in_specs=with_core(2),
        out_specs=in_vmem(slots),
        compiler_params=params(),
        cost_estimate=cost(choose.shape[0], choose.shape[1], width),
    )(core, choose, rows)
    return own, others


def project(core_ref, own_ref, piece_refs, weight_ref, hidden_ref, rows_ref, before):
    chips = core_ref.shape[0]
    count = len(piece_refs) // 2
    part = own_ref.shape[1] // (2 * chips)
    first = core_ref[0] == 0
    gate = upward = 0.0
    for index in range(2 * chips):
        chip, core = index // 2, index % 2
        column = slice(index * part, (index + 1) * part)
        of = slice(chip * part, (chip + 1) * part)
        values = [own_ref[:, column]]
        for piece in range(count):
            own, other = piece_refs[piece][:, of], piece_refs[count + piece][:, of]
            values.append(
                jnp.where(first, own, other) if core == 0 else jnp.where(first, other, own)
            )
        if all(value.shape[0] % 16 == 0 for value in values):
            at = 0
            for value in values:
                rows_ref[at : at + value.shape[0]] = value
                at += value.shape[0]
        else:
            joined = jnp.concatenate([value.astype(jnp.float32) for value in values])
            rows_ref[...] = joined.astype(jnp.bfloat16)
        rows = rows_ref[...]
        before(index)
        gate += lax.dot_general(
            rows, weight_ref[index, 0], CONTRACT_LAST, preferred_element_type=jnp.float32
        )
        upward += lax.dot_general(
            rows, weight_ref[index, 1], CONTRACT_LAST, preferred_element_type=jnp.float32
        )
    hidden_ref[...] = (gate / (1.0 + jnp.exp(-gate)) * upward).astype(jnp.bfloat16)


def up_kernel(core_ref, own_ref, *refs):
    *piece_refs, weight_ref, hidden_ref, rows_ref = refs
    project(core_ref, own_ref, piece_refs, weight_ref, hidden_ref, rows_ref, lambda index: None)


def first_up_kernel(core_ref, columns_ref, own_ref, *refs):
    *piece_refs, from_ref, hidden_ref, weight_ref, down_ref, rows_ref, sems = refs
    parts = weight_ref.shape[0]
    chips = down_ref.shape[0]
    part = weight_ref.shape[3]
    copies = [
        pltpu.make_async_copy(
            from_ref.at[0, 0:2, :, index * part : (index + 1) * part],
            weight_ref.at[index],
            sems.at[index],
        )
        for index in range(parts)
    ]
    for chip in range(chips):
        at = pl.multiple_of(columns_ref[0, chip] * part, part)
        copies.append(
            pltpu.make_async_copy(
                from_ref.at[0, 2, :, pl.ds(at, part)], down_ref.at[chip], sems.at[parts + chip]
            )
        )
    ahead = 3
    for copy in copies[:ahead]:
        copy.start()

    def before(index):
        copies[index].wait()
        if index + ahead < len(copies):
            copies[index + ahead].start()

    project(core_ref, own_ref, piece_refs, weight_ref, hidden_ref, rows_ref, before)
    for index in range(parts, len(copies)):
        before(index)


def first_up(core, columns, own, own_pieces, other_pieces, weights):
    chips = core.shape[0]
    total = own.shape[0] + sum(piece.shape[0] for piece in own_pieces)
    units, width = weights.shape[2:]
    part = width // (2 * chips)
    return pl.pallas_call(
        first_up_kernel,
        out_shape=[
            jax.ShapeDtypeStruct((total, units), jnp.bfloat16),
            pltpu.VMEM((2 * chips, 2, units, part), jnp.bfloat16),
            pltpu.VMEM((chips, units, part), jnp.bfloat16),
        ],
        in_specs=[pl.BlockSpec(memory_space=pltpu.SMEM)] * 2
        + in_vmem(2 * len(own_pieces) + 1)
        + [in_hbm()],
        out_specs=in_vmem(3),
        scratch_shapes=[
            pltpu.VMEM((total, part), jnp.bfloat16),
            pltpu.SemaphoreType.DMA((3 * chips,)),
        ],
        compiler_params=params(),
        cost_estimate=cost(total, width, 2 * units),
    )(core, columns, own, *own_pieces, *other_pieces, weights)


def up(core, own, own_pieces, other_pieces, weights):
    total, width = own.shape[0] + sum(piece.shape[0] for piece in own_pieces), own.shape[1]
    units, part = weights.shape[2:]
    return pl.pallas_call(
        up_kernel,
        out_shape=jax.ShapeDtypeStruct((total, units), jnp.bfloat16),
        in_specs=with_core(2 * len(own_pieces) + 2),
        out_specs=in_vmem(1)[0],
        scratch_shapes=[pltpu.VMEM((total, part), jnp.bfloat16)],
        compiler_params=params(),
        cost_estimate=cost(total, width, 2 * units),
    )(core, own, *own_pieces, *other_pieces, weights)


def down_kernel(columns_ref, hidden_ref, other_hidden_ref, weight_ref, other_ref, *out_refs):
    hidden, other_hidden = hidden_ref[...], other_hidden_ref[...]
    for shift, out_ref in enumerate(out_refs):
        total = jnp.dot(hidden, weight_ref[shift], preferred_element_type=jnp.float32)
        total += jnp.dot(
            other_hidden, other_ref[columns_ref[1, shift]], preferred_element_type=jnp.float32
        )
        out_ref[...] = total.astype(jnp.bfloat16)


def down(columns, hidden, other_hidden, weights, other_weights):
    chips, units, part = other_weights.shape
    rows = hidden.shape[0]
    return pl.pallas_call(
        down_kernel,
        out_shape=[jax.ShapeDtypeStruct((rows, part), jnp.bfloat16)] * chips,
        in_specs=with_core(4),
        out_specs=in_vmem(chips),
        compiler_params=params(),
        cost_estimate=cost(rows, 2 * units, chips * part),
    )(columns, hidden, other_hidden, weights, other_weights)


def unpack_kernel(weight_ref, *refs):
    *piece_refs, out_ref = refs
    rows = jnp.concatenate([ref[...].astype(jnp.float32) for ref in piece_refs])
    rows = rows.astype(jnp.bfloat16)
    weight = weight_ref[...]
    high = weight.astype(jnp.bfloat16)
    low = (weight - high.astype(jnp.float32)).astype(jnp.bfloat16)
    total = jnp.dot(high, rows, preferred_element_type=jnp.float32)
    total += jnp.dot(low, rows, preferred_element_type=jnp.float32)
    out_ref[...] = total.astype(jnp.bfloat16)


def unpack(weight, pieces):
    rows, part = weight.shape[0], pieces[0].shape[1]
    return pl.pallas_call(
        unpack_kernel,
        out_shape=jax.ShapeDtypeStruct((rows, part), jnp.bfloat16),
        in_specs=in_vmem(1 + len(pieces)),
        out_specs=in_vmem(1)[0],
        compiler_params=params(),
        cost_estimate=cost(rows, weight.shape[1], part),
    )(weight, *pieces)


def per_device(
    tokens, expert_ids, gate_weights, replica_pick, placement, slot_limit, expert_weights
):
    spans, rows, width = tokens.shape
    top = expert_ids.shape[2]
    ep = lax.axis_size("ep")
    tp = lax.axis_size("tp")
    chips = tp // 2
    part = width // tp
    capacity = rows * top * 5 // (4 * ep)
    few = ep <= 8
    own_slot = lax.axis_index("ep")
    own_chip = lax.axis_index("tp") // 2
    own_core = lax.axis_index("tp") % 2
    slot_range = jnp.arange(ep, dtype=jnp.int32)
    chip_range = jnp.arange(chips, dtype=jnp.int32)
    core = jnp.full((chips,), own_core, jnp.int32)
    chip_order = (own_chip + chip_range) % chips
    columns = jnp.stack([chip_order * 2 + own_core, chip_order])

    def along_ep(value, shift):
        return lax.ppermute(value, "ep", [(i, (i + shift) % ep) for i in range(ep)])

    def along_chips(value, shift):
        pairs = [
            (x * 2 + c, (x + shift) % chips * 2 + c) for x in range(chips) for c in range(2)
        ]
        return lax.ppermute(value, "tp", pairs)

    def along_cores(value):
        return lax.ppermute(value, "tp", [(i, i ^ 1) for i in range(tp)])

    def exchange(pieces, back):
        sign = -1 if back else 1
        if few:
            return [along_ep(piece, sign * (at + 1)) for at, piece in enumerate(pieces)]
        stacked = jnp.stack([pieces[0]] + pieces)
        placed = stacked[sign * (slot_range - own_slot) % ep]
        came = lax.all_to_all(placed, "ep", 0, 0, tiled=True)
        return list(came[(own_slot - sign * slot_range[1:]) % ep])

    weights = pltpu.with_memory_space_constraint(expert_weights, pltpu.HBM)
    arrived = {}
    for span in range(1, spans):
        sent = take(core, pltpu.with_memory_space_constraint(tokens, pltpu.HBM), (span,), 0, False)
        arrived[span] = (tokens[span], exchange([sent] * (ep - 1), False))

    slot, rank, kept_gates, kept = routes(
        placement, slot_limit, expert_ids, replica_pick, gate_weights
    )
    place = (slot[0] - own_slot) % ep * capacity + rank[0]
    place = jnp.where(kept[0], place, ep * capacity)
    hits = place[:, :, None] == jnp.arange(ep * capacity, dtype=jnp.int32)
    choose = jnp.any(hits, axis=1).astype(jnp.bfloat16).T
    own, others = pack(core, choose, tokens[0], ep)
    for_other = take(core, weights, (0, 2), 1, True)
    for_other, others = lax.optimization_barrier((for_other, others))
    other_down = along_cores(for_other)
    swapped = {}
    for span in range(1, spans):
        own_rows, pieces = arrived[span]
        both = (pieces, [along_cores(piece) for piece in pieces])
        same = 1 - core
        both, others, other_down, same, weights = lax.optimization_barrier(
            (both, others, other_down, same, weights)
        )
        arrived[span], swapped[span] = (own_rows, both[0]), both[1]
        same = along_cores(same)
    arrived[0] = (own, exchange(others, False))

    kept_weights = []

    def finish(span, after):
        own, pieces = arrived[span]
        if after is not None:
            own, pieces, after = lax.optimization_barrier((own, pieces, after))
        others = swapped.get(span) or [along_cores(piece) for piece in pieces]
        if after is None:
            hidden, *loaded = first_up(
                core,
                columns,
                own,
                pieces,
                others,
                pltpu.with_memory_space_constraint(weights, pltpu.HBM),
            )
            kept_weights.extend(loaded)
            hidden, core_there = lax.optimization_barrier((hidden, same))
        else:
            hidden = up(after[1], own, pieces, others, kept_weights[0])
            core_there = core
        sums = down(columns, hidden, along_cores(hidden), kept_weights[1], other_down)
        came = [along_chips(sums[shift], shift) for shift in range(1, chips)]
        totals = []
        count = own.shape[0]
        for piece in range(ep):
            at = slice(piece * count, (piece + 1) * count)
            total = sums[0][at].astype(jnp.float32)
            for value in came:
                total = total + value[at].astype(jnp.float32)
            totals.append(total.astype(jnp.bfloat16))
        return [totals[0]] + exchange(totals[1:], True), (sums, core_there)

    returned = {}
    hidden = None
    for span in list(range(1, spans)) + [0]:
        returned[span], hidden = finish(span, hidden)

    old_table = placement[0]
    outs = []
    for span in range(spans):
        if span == 0:
            weight = jnp.sum(jnp.where(hits, kept_gates[0][:, :, None], 0.0), axis=1)
            outs.append(unpack(weight, returned[0]))
            continue
        serves = placement[span][:, None] == old_table[None, :]
        serving = jnp.min(jnp.where(serves, slot_range, ep), axis=1)
        served = jnp.sum(
            jnp.where(slot[span][:, :, None] == slot_range, (serving - own_slot) % ep, 0), axis=2
        )
        combined = jnp.zeros((rows, part), jnp.float32)
        for at in range(ep):
            share = jnp.sum(jnp.where(served == at, kept_gates[span], 0.0), axis=1)[:, None]
            value = share * returned[span][at].astype(jnp.float32)
            combined = combined + jnp.where(share != 0, value, 0.0)
        outs.append(combined.astype(jnp.bfloat16))
    return jnp.stack(outs)


def solution(mesh):
    placed = (
        P(None, ("groups", "ep"), None),
        P(None, ("groups", "ep"), None),
        P(None, ("groups", "ep"), None),
        P(None, ("groups", "ep"), None),
        P(),
        P(),
        P("ep", None, "tp", None),
    )
    return jax.shard_map(
        per_device,
        mesh=mesh,
        in_specs=placed,
        out_specs=P(None, ("groups", "ep"), "tp"),
        check_vma=False,
    )
```

```python
import functools

import jax
import jax.numpy as jnp
from jax import lax
from jax.experimental import pallas as pl
from jax.experimental.pallas import tpu as pltpu
from jax.sharding import PartitionSpec as P

VMEM_LIMIT = 32 * 1024 * 1024
CONTRACT_LAST = (((1,), (1,)), ((), ()))


def routes(placement, limits, chosen_ids, pick_values, gates):
    spans, rows, top = chosen_ids.shape
    slots = placement.shape[1]
    slot_range = jnp.arange(slots, dtype=jnp.int32)
    same = placement[:, :, None] == placement[:, None, :]
    before = slot_range[None, :] < slot_range[:, None]
    turn = jnp.sum((same & before).astype(jnp.int32), axis=2)
    flat_ids = chosen_ids.reshape(spans, rows * top)
    holders = flat_ids[:, :, None] == placement[:, None, :]
    count = jnp.sum(holders.astype(jnp.int32), axis=2)
    wanted = pick_values.reshape(spans, rows * top) % count
    onehot = holders & (turn[:, None, :] == wanted[:, :, None])
    slot = jnp.sum(jnp.where(onehot, slot_range, 0), axis=2)
    limit = jnp.sum(jnp.where(onehot, limits, 0), axis=2)
    order = jnp.arange(rows * top, dtype=jnp.int32)
    ahead = (slot[:, :, None] == slot[:, None, :]) & (order[None, :] < order[:, None])
    rank = jnp.sum(ahead.astype(jnp.int32), axis=2)
    kept = rank < limit
    shape = (spans, rows, top)
    return (
        slot.reshape(shape),
        rank.reshape(shape),
        jnp.where(kept.reshape(shape), gates, 0.0),
        kept.reshape(shape),
    )


def in_vmem(count):
    return [pl.BlockSpec(memory_space=pltpu.VMEM)] * count


def with_core(count):
    return [pl.BlockSpec(memory_space=pltpu.SMEM)] + in_vmem(count)


def params():
    return pltpu.CompilerParams(vmem_limit_bytes=VMEM_LIMIT)


def cost(rows, width, units):
    return pl.CostEstimate(flops=2 * rows, bytes_accessed=2 * rows, transcendentals=0)


def in_hbm():
    return pl.BlockSpec(memory_space=pltpu.HBM)


def take_kernel(lead, side, core_ref, from_ref, out_ref, sems):
    chips = core_ref.shape[0]
    part = from_ref.shape[-1] // (2 * chips)
    copies = []
    for chip in range(chips):
        core = core_ref[chip] if side == 0 else 1 - core_ref[chip]
        at = pl.multiple_of((2 * chip + core) * part, part)
        if len(out_ref.shape) == 3:
            to = out_ref.at[chip]
        else:
            to = out_ref.at[:, chip * part : (chip + 1) * part]
        copies.append(
            pltpu.make_async_copy(from_ref.at[*lead, :, pl.ds(at, part)], to, sems.at[chip])
        )
    for copy in copies:
        copy.start()
    for copy in copies:
        copy.wait()


def take(core, values, lead, side, stacked):
    chips = core.shape[0]
    rows, width = values.shape[-2:]
    part = width // (2 * chips)
    shape = (chips, rows, part) if stacked else (rows, chips * part)
    return pl.pallas_call(
        functools.partial(take_kernel, lead, side),
        out_shape=jax.ShapeDtypeStruct(shape, jnp.bfloat16),
        in_specs=[pl.BlockSpec(memory_space=pltpu.SMEM), in_hbm()],
        out_specs=in_vmem(1)[0],
        scratch_shapes=[pltpu.SemaphoreType.DMA((chips,))],
        compiler_params=params(),
        cost_estimate=cost(rows, width, 1),
    )(core, values)


def pack_kernel(core_ref, choose_ref, rows_ref, own_ref, *out_refs):
    chips = core_ref.shape[0]
    count = own_ref.shape[0]
    part = own_ref.shape[1] // (2 * chips)
    first = core_ref[0] == 0
    choose = choose_ref[...]
    for chip in range(chips):
        of = 2 * chip * part
        low = jnp.dot(
            choose, rows_ref[:, of : of + part], preferred_element_type=jnp.float32
        )
        high = jnp.dot(
            choose, rows_ref[:, of + part : of + 2 * part], preferred_element_type=jnp.float32
        )
        own_ref[:, of : of + part] = low[:count].astype(jnp.bfloat16)
        own_ref[:, of + part : of + 2 * part] = high[:count].astype(jnp.bfloat16)
        sent = jnp.where(first, low, high)
        for index, out_ref in enumerate(out_refs):
            at = (index + 1) * count
            out_ref[:, chip * part : (chip + 1) * part] = sent[at : at + count].astype(jnp.bfloat16)


def pack(core, choose, rows, slots):
    count = choose.shape[0] // slots
    width = rows.shape[1]
    outs = [jax.ShapeDtypeStruct((count, width), jnp.bfloat16)]
    outs += [jax.ShapeDtypeStruct((count, width // 2), jnp.bfloat16)] * (slots - 1)
    own, *others = pl.pallas_call(
        pack_kernel,
        out_shape=outs,
        in_specs=with_core(2),
        out_specs=in_vmem(slots),
        compiler_params=params(),
        cost_estimate=cost(choose.shape[0], choose.shape[1], width),
    )(core, choose, rows)
    return own, others


def project(core_ref, own_ref, piece_refs, weight_ref, hidden_ref, rows_ref, before):
    chips = core_ref.shape[0]
    count = len(piece_refs) // 2
    part = own_ref.shape[1] // (2 * chips)
    first = core_ref[0] == 0
    gate = upward = 0.0
    for index in range(2 * chips):
        chip, core = index // 2, index % 2
        column = slice(index * part, (index + 1) * part)
        of = slice(chip * part, (chip + 1) * part)
        values = [own_ref[:, column]]
        for piece in range(count):
            own, other = piece_refs[piece][:, of], piece_refs[count + piece][:, of]
            values.append(
                jnp.where(first, own, other) if core == 0 else jnp.where(first, other, own)
            )
        if all(value.shape[0] % 16 == 0 for value in values):
            at = 0
            for value in values:
                rows_ref[at : at + value.shape[0]] = value
                at += value.shape[0]
        else:
            joined = jnp.concatenate([value.astype(jnp.float32) for value in values])
            rows_ref[...] = joined.astype(jnp.bfloat16)
        rows = rows_ref[...]
        before(index)
        gate += lax.dot_general(
            rows, weight_ref[index, 0], CONTRACT_LAST, preferred_element_type=jnp.float32
        )
        upward += lax.dot_general(
            rows, weight_ref[index, 1], CONTRACT_LAST, preferred_element_type=jnp.float32
        )
    hidden_ref[...] = (gate / (1.0 + jnp.exp(-gate)) * upward).astype(jnp.bfloat16)


def up_kernel(core_ref, own_ref, *refs):
    *piece_refs, weight_ref, hidden_ref, rows_ref = refs
    project(core_ref, own_ref, piece_refs, weight_ref, hidden_ref, rows_ref, lambda index: None)


def first_up_kernel(core_ref, columns_ref, own_ref, *refs):
    *piece_refs, from_ref, hidden_ref, weight_ref, down_ref, rows_ref, sems = refs
    parts = weight_ref.shape[0]
    chips = down_ref.shape[0]
    part = weight_ref.shape[3]
    copies = [
        pltpu.make_async_copy(
            from_ref.at[0, 0:2, :, index * part : (index + 1) * part],
            weight_ref.at[index],
            sems.at[index],
        )
        for index in range(parts)
    ]
    for chip in range(chips):
        at = pl.multiple_of(columns_ref[0, chip] * part, part)
        copies.append(
            pltpu.make_async_copy(
                from_ref.at[0, 2, :, pl.ds(at, part)], down_ref.at[chip], sems.at[parts + chip]
            )
        )
    ahead = 3
    for copy in copies[:ahead]:
        copy.start()

    def before(index):
        copies[index].wait()
        if index + ahead < len(copies):
            copies[index + ahead].start()

    project(core_ref, own_ref, piece_refs, weight_ref, hidden_ref, rows_ref, before)
    for index in range(parts, len(copies)):
        before(index)


def first_up(core, columns, own, own_pieces, other_pieces, weights):
    chips = core.shape[0]
    total = own.shape[0] + sum(piece.shape[0] for piece in own_pieces)
    units, width = weights.shape[2:]
    part = width // (2 * chips)
    return pl.pallas_call(
        first_up_kernel,
        out_shape=[
            jax.ShapeDtypeStruct((total, units), jnp.bfloat16),
            pltpu.VMEM((2 * chips, 2, units, part), jnp.bfloat16),
            pltpu.VMEM((chips, units, part), jnp.bfloat16),
        ],
        in_specs=[pl.BlockSpec(memory_space=pltpu.SMEM)] * 2
        + in_vmem(2 * len(own_pieces) + 1)
        + [in_hbm()],
        out_specs=in_vmem(3),
        scratch_shapes=[
            pltpu.VMEM((total, part), jnp.bfloat16),
            pltpu.SemaphoreType.DMA((3 * chips,)),
        ],
        compiler_params=params(),
        cost_estimate=cost(total, width, 2 * units),
    )(core, columns, own, *own_pieces, *other_pieces, weights)


def up(core, own, own_pieces, other_pieces, weights):
    total, width = own.shape[0] + sum(piece.shape[0] for piece in own_pieces), own.shape[1]
    units, part = weights.shape[2:]
    return pl.pallas_call(
        up_kernel,
        out_shape=jax.ShapeDtypeStruct((total, units), jnp.bfloat16),
        in_specs=with_core(2 * len(own_pieces) + 2),
        out_specs=in_vmem(1)[0],
        scratch_shapes=[pltpu.VMEM((total, part), jnp.bfloat16)],
        compiler_params=params(),
        cost_estimate=cost(total, width, 2 * units),
    )(core, own, *own_pieces, *other_pieces, weights)


def down_kernel(columns_ref, hidden_ref, other_hidden_ref, weight_ref, other_ref, *out_refs):
    hidden, other_hidden = hidden_ref[...], other_hidden_ref[...]
    for shift, out_ref in enumerate(out_refs):
        total = jnp.dot(hidden, weight_ref[shift], preferred_element_type=jnp.float32)
        total += jnp.dot(
            other_hidden, other_ref[columns_ref[1, shift]], preferred_element_type=jnp.float32
        )
        out_ref[...] = total.astype(jnp.bfloat16)


def down(columns, hidden, other_hidden, weights, other_weights):
    chips, units, part = other_weights.shape
    rows = hidden.shape[0]
    return pl.pallas_call(
        down_kernel,
        out_shape=[jax.ShapeDtypeStruct((rows, part), jnp.bfloat16)] * chips,
        in_specs=with_core(4),
        out_specs=in_vmem(chips),
        compiler_params=params(),
        cost_estimate=cost(rows, 2 * units, chips * part),
    )(columns, hidden, other_hidden, weights, other_weights)


def unpack_kernel(weight_ref, *refs):
    *piece_refs, rest_ref, out_ref = refs
    rows = jnp.concatenate([ref[...].astype(jnp.float32) for ref in piece_refs])
    rows = rows.astype(jnp.bfloat16)
    weight = weight_ref[...]
    high = weight.astype(jnp.bfloat16)
    low = (weight - high.astype(jnp.float32)).astype(jnp.bfloat16)
    total = jnp.dot(high, rows, preferred_element_type=jnp.float32)
    total += jnp.dot(low, rows, preferred_element_type=jnp.float32)
    out_ref[0] = total.astype(jnp.bfloat16)
    out_ref[1:] = rest_ref[...]


def unpack(weight, pieces, rest):
    rows, part = weight.shape[0], pieces[0].shape[1]
    return pl.pallas_call(
        unpack_kernel,
        out_shape=jax.ShapeDtypeStruct((rest.shape[0] + 1, rows, part), jnp.bfloat16),
        in_specs=in_vmem(2 + len(pieces)),
        out_specs=in_vmem(1)[0],
        compiler_params=params(),
        cost_estimate=cost(rows, weight.shape[1], part),
    )(weight, *pieces, rest)


def per_device(
    tokens, expert_ids, gate_weights, replica_pick, placement, slot_limit, expert_weights
):
    spans, rows, width = tokens.shape
    top = expert_ids.shape[2]
    ep = lax.axis_size("ep")
    tp = lax.axis_size("tp")
    chips = tp // 2
    part = width // tp
    capacity = rows * top * 5 // (4 * ep)
    few = ep <= 8
    own_slot = lax.axis_index("ep")
    own_chip = lax.axis_index("tp") // 2
    own_core = lax.axis_index("tp") % 2
    slot_range = jnp.arange(ep, dtype=jnp.int32)
    chip_range = jnp.arange(chips, dtype=jnp.int32)
    core = jnp.full((chips,), own_core, jnp.int32)
    chip_order = (own_chip + chip_range) % chips
    columns = jnp.stack([chip_order * 2 + own_core, chip_order])

    def along_ep(value, shift):
        return lax.ppermute(value, "ep", [(i, (i + shift) % ep) for i in range(ep)])

    def along_chips(value, shift):
        pairs = [
            (x * 2 + c, (x + shift) % chips * 2 + c) for x in range(chips) for c in range(2)
        ]
        return lax.ppermute(value, "tp", pairs)

    def along_cores(value):
        return lax.ppermute(value, "tp", [(i, i ^ 1) for i in range(tp)])

    def exchange(pieces, back):
        sign = -1 if back else 1
        if few:
            return [along_ep(piece, sign * (at + 1)) for at, piece in enumerate(pieces)]
        stacked = jnp.stack([pieces[0]] + pieces)
        placed = stacked[sign * (slot_range - own_slot) % ep]
        came = lax.all_to_all(placed, "ep", 0, 0, tiled=True)
        return list(came[(own_slot - sign * slot_range[1:]) % ep])

    weights = pltpu.with_memory_space_constraint(expert_weights, pltpu.HBM)
    arrived = {}
    for span in range(1, spans):
        sent = take(core, pltpu.with_memory_space_constraint(tokens, pltpu.HBM), (span,), 0, False)
        arrived[span] = (tokens[span], exchange([sent] * (ep - 1), False))

    slot, rank, kept_gates, kept = routes(
        placement, slot_limit, expert_ids, replica_pick, gate_weights
    )
    place = (slot[0] - own_slot) % ep * capacity + rank[0]
    place = jnp.where(kept[0], place, ep * capacity)
    hits = place[:, :, None] == jnp.arange(ep * capacity, dtype=jnp.int32)
    choose = jnp.any(hits, axis=1).astype(jnp.bfloat16).T
    own, others = pack(core, choose, tokens[0], ep)
    for_other = take(core, weights, (0, 2), 1, True)
    for_other, others = lax.optimization_barrier((for_other, others))
    other_down = along_cores(for_other)
    swapped = {}
    for span in range(1, spans):
        own_rows, pieces = arrived[span]
        both = (pieces, [along_cores(piece) for piece in pieces])
        same = 1 - core
        both, others, other_down, same, weights = lax.optimization_barrier(
            (both, others, other_down, same, weights)
        )
        arrived[span], swapped[span] = (own_rows, both[0]), both[1]
        same = along_cores(same)
    arrived[0] = (own, exchange(others, False))

    kept_weights = []

    def finish(span, after):
        own, pieces = arrived[span]
        if after is not None:
            own, pieces, after = lax.optimization_barrier((own, pieces, after))
        others = swapped.get(span) or [along_cores(piece) for piece in pieces]
        if after is None:
            hidden, *loaded = first_up(
                core,
                columns,
                own,
                pieces,
                others,
                pltpu.with_memory_space_constraint(weights, pltpu.HBM),
            )
            kept_weights.extend(loaded)
            hidden, core_there = lax.optimization_barrier((hidden, same))
        else:
            hidden = up(after[1], own, pieces, others, kept_weights[0])
            core_there = core
        sums = down(columns, hidden, along_cores(hidden), kept_weights[1], other_down)
        came = [along_chips(sums[shift], shift) for shift in range(1, chips)]
        totals = []
        count = own.shape[0]
        for piece in range(ep):
            at = slice(piece * count, (piece + 1) * count)
            total = sums[0][at].astype(jnp.float32)
            for value in came:
                total = total + value[at].astype(jnp.float32)
            totals.append(total.astype(jnp.bfloat16))
        return [totals[0]] + exchange(totals[1:], True), (sums, core_there)

    returned = {}
    hidden = None
    for span in list(range(1, spans)) + [0]:
        returned[span], hidden = finish(span, hidden)

    old_table = placement[0]
    outs = []
    for span in range(1, spans):
        serves = placement[span][:, None] == old_table[None, :]
        serving = jnp.min(jnp.where(serves, slot_range, ep), axis=1)
        served = jnp.sum(
            jnp.where(slot[span][:, :, None] == slot_range, (serving - own_slot) % ep, 0), axis=2
        )
        combined = jnp.zeros((rows, part), jnp.float32)
        for at in range(ep):
            share = jnp.sum(jnp.where(served == at, kept_gates[span], 0.0), axis=1)[:, None]
            value = share * returned[span][at].astype(jnp.float32)
            combined = combined + jnp.where(share != 0, value, 0.0)
        outs.append(combined.astype(jnp.bfloat16))
    weight = jnp.sum(jnp.where(hits, kept_gates[0][:, :, None], 0.0), axis=1)
    return unpack(weight, returned[0], jnp.stack(outs))


def solution(mesh):
    placed = (
        P(None, ("groups", "ep"), None),
        P(None, ("groups", "ep"), None),
        P(None, ("groups", "ep"), None),
        P(None, ("groups", "ep"), None),
        P(),
        P(),
        P("ep", None, "tp", None),
    )
    return jax.shard_map(
        per_device,
        mesh=mesh,
        in_specs=placed,
        out_specs=P(None, ("groups", "ep"), "tp"),
        check_vma=False,
    )
```
